32 devices in a mesh: groups: 2 (over x), member: 2 (over core), tile: 8 (over z, y).
Axes of the slice: x: 2, y: 2, z: 4, core: 2. Of those that a mesh axis runs over, the one named last changes fastest.
Arguments:
- state: float32 [8, 4, 4, 512, 256], P(('groups', 'member'), None, None, 'tile'), parts along dimension 0, may hold values from -6 to 6
- perturbation: float32 [8, 4, 4, 512, 256], P(('groups', 'member'), None, None, 'tile'), parts along dimension 0, may hold values from -2 to 2
- ancestors: int32 [8], P('groups'), parts along dimension 0, may hold values from 0 to 3, as said below
Outputs:
- evolved: float32 [8, 4, 4, 512, 256], P(('groups', 'member'), None, None, 'tile'), parts along dimension 0
- observable: float32 [8], P(('groups', 'member')), parts along dimension 0
The draws below stay inside these ranges and needn't reach their ends.
There are 2 independent parts, one for each index of `groups`. The reference program is written for one: setup_inputs(seed, part) draws one part's arguments, and reference() takes and returns one part's arrays. A program takes and returns all parts, laid end to end along the dimension named above; each array names one. Nothing has to cross between parts.
Inputs may be any that keep to these rules, and one draw needn't show every extreme that they name: `ancestors`: surviving slots name themselves; every other slot names a surviving slot; at least two slots survive and at least one does not.
All inputs are finite; a program needn't handle non-finite values.
Results may differ from the reference program's by a relative error of at most 0.00002.
Values sent between devices are 32-bit elements; how exact they have to be, the bound alone decides.
No kernel may reach another device: no remote copies, remote signals or barrier semaphores. Data moves between devices by JAX's collectives and lax.ppermute only.
A program may use at most 64 MiB of HBM per device.

```python
import jax
import jax.numpy as jnp

COLUMNS = 256
LEVELS = 4
FIELDS = 4
STEPS_EACH = 2
ENSEMBLE_SIZE = 4
ROWS = 512


def draw_ancestors(key, part):
    key_order = jax.random.fold_in(key, 11)
    count_key = jax.random.fold_in(key, 12)
    picking_key = jax.random.fold_in(key, 13)
    order = jax.random.permutation(key_order, ENSEMBLE_SIZE).astype(jnp.int32)
    member_ranks = jnp.argsort(order, stable=True).astype(jnp.int32)
    kept_members = jax.random.randint(count_key, (), 2, ENSEMBLE_SIZE, dtype=jnp.int32)
    living_members = member_ranks < kept_members
    chosen_members = jax.random.randint(picking_key, (ENSEMBLE_SIZE,), 0, kept_members, dtype=jnp.int32)
    sources = jnp.take(order, chosen_members)
    return jnp.where(living_members, jnp.arange(ENSEMBLE_SIZE, dtype=jnp.int32), sources).astype(jnp.int32)


def block_scale(rng, extent, cuts, least, high):
    gain, own = 1.0, jax.random.fold_in(rng, 6)
    for dim, shards_of in cuts:
        steps = jnp.exp(jax.random.uniform(jax.random.fold_in(own, dim), (shards_of,), jnp.float32, least / len(cuts), high / len(cuts)))
        gain = gain * jnp.repeat(steps, extent[dim] // shards_of).reshape([-1 if axis == dim else 1 for axis in range(len(extent))])
    return gain


def normal_values(key, extent, scale, reach, split=(), held_as=jnp.bfloat16):
    array = scale * jax.random.normal(key, extent, jnp.float32)
    if split:
        array = array * block_scale(key, extent, split, -0.22, 0.18)
    return jnp.clip(array, -reach, reach).astype(held_as)


def setup_inputs(seed: int = 0, part: int = 0) -> dict:
    arg_keys = jax.random.split(jax.random.key(seed), 4)
    part_keys = jax.random.split(jax.random.fold_in(arg_keys[3], part), 4)
    state = normal_values(part_keys[0], (ENSEMBLE_SIZE, FIELDS, LEVELS, ROWS, COLUMNS), 1.0, 6.0, ((0, 2), (3, 8)), jnp.float32)
    perturbation = normal_values(part_keys[1], (ENSEMBLE_SIZE, FIELDS, LEVELS, ROWS, COLUMNS), 0.3, 2.0, ((0, 2), (3, 8)), jnp.float32)
    ancestors = draw_ancestors(jax.random.fold_in(jax.random.fold_in(arg_keys[3], part), 71), part)
    return {"state": state, "perturbation": perturbation, "ancestors": ancestors}


TIME_STEP = 0.15
DIFFUSION = 0.2
MIXING = 0.1
CORIOLIS = 0.5
BUOYANCY_GAIN = 0.3
STRATIFICATION = 0.3
SATURATION = 0.5
LATENT = 0.5


def advance_core(padded):
    centre = padded[:, :, :, 2:-2, :]
    north_one = padded[:, :, :, 3:-1, :]
    south_one = padded[:, :, :, 1:-3, :]
    north_two = padded[:, :, :, 4:, :]
    south_two = padded[:, :, :, :-4, :]
    east_one = jnp.roll(centre, -1, axis=4)
    west_one = jnp.roll(centre, 1, axis=4)
    east_two = jnp.roll(centre, -2, axis=4)
    west_two = jnp.roll(centre, 2, axis=4)
    slope_y = (8.0 * (north_one - south_one) - (north_two - south_two)) / 12.0
    slope_x = (8.0 * (east_one - west_one) - (east_two - west_two)) / 12.0
    laplace = north_one + south_one + east_one + west_one - 4.0 * centre
    upper = jnp.concatenate([centre[:, :, 1:], centre[:, :, -1:]], axis=2)
    lower = jnp.concatenate([centre[:, :, :1], centre[:, :, :-1]], axis=2)
    vertical = upper + lower - 2.0 * centre
    east_wind = centre[:, 0:1]
    north_wind = centre[:, 1:2]
    buoyancy = centre[:, 2:3]
    tendency = -(east_wind * slope_x + north_wind * slope_y) + DIFFUSION * laplace + MIXING * vertical
    forcing = jnp.concatenate([CORIOLIS * north_wind, -CORIOLIS * east_wind + BUOYANCY_GAIN * buoyancy,
                               -STRATIFICATION * north_wind, jnp.zeros_like(north_wind)], axis=1)
    updated = centre + TIME_STEP * (tendency + forcing)
    buoyancy_new = updated[:, 2:3]
    moisture = updated[:, 3:4]
    excess = jnp.maximum(moisture - SATURATION * jnp.exp(0.1 * buoyancy_new), 0.0)
    return jnp.concatenate([updated[:, 0:2], buoyancy_new + LATENT * excess, moisture - excess], axis=1)


def advance_all(fields):
    for number in range(STEPS_EACH):
        fields = advance_core(jnp.pad(fields, ((0, 0), (0, 0), (0, 0), (2, 2), (0, 0))))
    return fields


def reference(state, perturbation, ancestors):
    fields = advance_all(state)
    fields = jnp.take(fields, ancestors.astype(jnp.int32), axis=0) + perturbation
    fields = advance_all(fields)
    rows_all = fields.shape[3]
    latitude = jnp.arange(rows_all).astype(jnp.float32)
    weight = 1.0 + 2.0 * latitude / (rows_all - 1)
    buoyancy = fields[:, 2]
    total = jnp.sum(weight[:, None] * buoyancy * buoyancy, axis=(1, 2, 3))
    observable = total / (fields.shape[2] * rows_all * fields.shape[4])
    return fields, observable
```

```python
import functools

import jax
import jax.numpy as jnp
from jax import lax
from jax.experimental import pallas as pl
from jax.experimental.pallas import tpu as pltpu
from jax.sharding import PartitionSpec as P

STEPS_EACH = 2
TIME_STEP = 0.15
DIFFUSION = 0.2
MIXING = 0.1
CORIOLIS = 0.5
BUOYANCY_GAIN = 0.3
STRATIFICATION = 0.3
SATURATION = 0.5
LATENT = 0.5

LANES = 128
TILE = 8
REACH = 2
DEEP = 4 * REACH
SHALLOW = 2 * REACH
STRIP = 24
BAND = 16

KEEP = 1.0 - TIME_STEP * (4.0 * DIFFUSION + 2.0 * MIXING)
SPREAD = TIME_STEP * DIFFUSION
LIFT = TIME_STEP * MIXING
NEAR = TIME_STEP * 8.0 / 12.0
FAR = TIME_STEP / 12.0


def shifted(parts, by):
    lane = lax.broadcasted_iota(jnp.int32, parts[0].shape, 1)
    turned = [pltpu.roll(part, (-by) % LANES, 1) for part in parts]
    count = len(parts)
    if by > 0:
        return [jnp.where(lane >= LANES - by, turned[(h + 1) % count], turned[h]) for h in range(count)]
    return [jnp.where(lane < -by, turned[(h - 1) % count], turned[h]) for h in range(count)]


def advance_tile(load, levels, halves, store):
    for l in range(levels):
        up, down = min(l + 1, levels - 1), max(l - 1, 0)
        centre = [[load(f, l, h, 0) for h in range(halves)] for f in range(4)]
        winds = []
        for h in range(halves):
            e, n = centre[0][h], centre[1][h]
            en, nn = NEAR * e, NEAR * n
            winds.append((SPREAD - en, SPREAD + en, FAR * e, SPREAD - nn, SPREAD + nn, FAR * n))
        updated = []
        for f in range(4):
            c = centre[f]
            e1, w1, e2, w2 = shifted(c, 1), shifted(c, -1), shifted(c, 2), shifted(c, -2)
            row = []
            for h in range(halves):
                ae, aw, ax, an, as_, ay = winds[h]
                new = KEEP * c[h] + LIFT * (load(f, up, h, 0) + load(f, down, h, 0))
                new += ae * e1[h] + aw * w1[h] + ax * (e2[h] - w2[h])
                new += an * load(f, l, h, 1) + as_ * load(f, l, h, -1)
                new += ay * (load(f, l, h, 2) - load(f, l, h, -2))
                row.append(new)
            updated.append(row)
        for h in range(halves):
            e, n, b = centre[0][h], centre[1][h], centre[2][h]
            turn = (TIME_STEP * CORIOLIS) * n
            store(0, l, h, updated[0][h] + turn)
            store(1, l, h, updated[1][h] - (TIME_STEP * CORIOLIS) * e + (TIME_STEP * BUOYANCY_GAIN) * b)
            b_new = updated[2][h] - (TIME_STEP * STRATIFICATION) * n
            q_new = updated[3][h]
            excess = jnp.maximum(q_new - SATURATION * jnp.exp(0.1 * b_new), 0.0)
            store(2, l, h, b_new + LATENT * excess)
            store(3, l, h, q_new - excess)


def loader(ref, lead, start):
    def load(f, l, h, shift):
        return ref[(*lead, f, l, h, pl.ds(start + shift, TILE), slice(None))]

    return load


def latitude(first_row, total_rows):
    rows = first_row + lax.broadcasted_iota(jnp.int32, (TILE, LANES), 0)
    return 1.0 + (2.0 / (total_rows - 1)) * rows.astype(jnp.float32)


def half(h):
    return pl.ds(h * LANES, LANES)


def interior_kernel(dims, ancestors, own, other, pert, fields, sums, kept, late, first, second, noise, sems):
    members, levels, rows, halves, total_rows = dims
    owner = lax.axis_index("member")
    tile = lax.axis_index("tile")
    top = rows + TILE

    def state_copy(source, number, m, h):
        return pltpu.make_async_copy(
            source.at[number, :, :, :, half(h)],
            first.at[m, :, :, h, pl.ds(TILE, rows), :],
            sems.at[m, h],
        )

    def pert_copy(m, h):
        return pltpu.make_async_copy(
            pert.at[m, :, :, :, half(h)], noise.at[m, :, :, h, pl.ds(TILE, rows), :], sems.at[members + m, h]
        )

    def out_copy(m, h):
        return pltpu.make_async_copy(
            first.at[m, :, :, h, pl.ds(2 * TILE, rows - 2 * TILE), :],
            fields.at[m, :, :, pl.ds(TILE, rows - 2 * TILE), half(h)],
            sems.at[2 * members + m, h],
        )

    for m in range(members):
        source = ancestors[owner * members + m]
        here = lax.div(source, members) == owner
        number = lax.rem(source, members)

        @pl.when(here)
        def _():
            for h in range(halves):
                state_copy(own, number, m, h).start()

        @pl.when(jnp.logical_not(here))
        def _():
            for h in range(halves):
                state_copy(other, number, m, h).start()

    for m in range(members):
        for h in range(halves):
            pert_copy(m, h).start()

    def sweep(source, target, m, start, tiles, post=None):
        def one(i, carry):
            r = start + i * TILE

            def store(f, l, h, value):
                if post is not None:
                    value = post(f, l, h, r, value)
                target[m, f, l, h, pl.ds(r, TILE), :] = value

            advance_tile(loader(source, (m,), r), levels, halves, store)
            return carry

        lax.fori_loop(0, tiles, one, 0)

    for m in range(members):
        for h in range(halves):
            state_copy(own, 0, m, h).wait()
        sweep(first, second, m, TILE + REACH, rows // TILE)
        for h in range(halves):
            pert_copy(m, h).wait()
        sweep(
            second,
            first,
            m,
            TILE + 2 * REACH,
            rows // TILE - 1,
            post=lambda f, l, h, r, value: value + noise[m, f, l, h, pl.ds(r, TILE), :],
        )
        for f in range(4):
            for l in range(levels):
                for h in range(halves):
                    kept[m, f, l, 0, h] = first[m, f, l, h, pl.ds(TILE + 4, 8), :]
                    kept[m, f, l, 1, h] = first[m, f, l, h, pl.ds(top - 8 - 4, 8), :]
        sweep(first, second, m, TILE + 3 * REACH, rows // TILE - 1)
        for f in range(4):
            for l in range(levels):
                for h in range(halves):
                    late[m, f, l, 0, h] = second[m, f, l, h, pl.ds(TILE + 6, 8), :]
                    late[m, f, l, 1, h] = second[m, f, l, h, pl.ds(top - 8 - 6, 8), :]

        def last(i, total):
            r = 2 * TILE + i * TILE
            weight = latitude(tile * rows + r - TILE, total_rows)
            squares = []

            def store(f, l, h, value):
                first[m, f, l, h, pl.ds(r, TILE), :] = value
                if f == 2:
                    squares.append(value * value)

            advance_tile(loader(second, (m,), r), levels, halves, store)
            return total + weight * sum(squares)

        sums[m] = lax.fori_loop(0, rows // TILE - 2, last, jnp.zeros((TILE, LANES), jnp.float32))
        for h in range(halves):
            out_copy(m, h).start()
    for m in range(members):
        for h in range(halves):
            out_copy(m, h).wait()


def early_edge_kernel(dims, ancestors, own, other, own_pair, own_cross, other_pair, other_cross, early, first, second, sems):
    members, levels, rows, halves, total_rows = dims
    owner = lax.axis_index("member")
    tile = lax.axis_index("tile")
    last_tile = lax.axis_size("tile") - 1
    odd = lax.rem(tile, 2) == 1

    def place(source, number, m, side, begin, h, local):
        return pltpu.make_async_copy(
            source.at[number, :, :, pl.ds(begin, TILE), half(h)],
            first.at[m, :, :, side, h, pl.ds(local, TILE), :],
            sems.at[m, side, local // TILE, h],
        )

    for m in range(members):
        source = ancestors[owner * members + m]
        here = lax.div(source, members) == owner
        number = lax.rem(source, members)

        def bring(state, low, high):
            for h in range(halves):
                place(low, number, m, 0, 0, h, 0).start()
                place(state, number, m, 0, 0, h, TILE).start()
                place(state, number, m, 1, rows - TILE, h, 0).start()
                place(high, number, m, 1, 0, h, TILE).start()

        for chosen, state, pair, cross in (
            (here, own, own_pair, own_cross),
            (jnp.logical_not(here), other, other_pair, other_cross),
        ):
            for parity, low, high in ((odd, pair, cross), (jnp.logical_not(odd), cross, pair)):

                @pl.when(jnp.logical_and(chosen, parity))
                def _():
                    bring(state, low, high)

    for m in range(members):
        for side in range(2):
            for h in range(halves):
                for local in (0, TILE):
                    place(own_pair, 0, m, side, 0, h, local).wait()

    outside = (tile == 0, tile == last_tile)

    def blank(ref, begin):
        def clear(side, start):
            for m in range(members):
                for f in range(4):
                    for l in range(levels):
                        for h in range(halves):
                            ref[m, f, l, side, h, pl.ds(start, TILE), :] = jnp.zeros((TILE, LANES), jnp.float32)

        @pl.when(outside[0])
        def _():
            clear(0, begin[0])

        @pl.when(outside[1])
        def _():
            clear(1, begin[1])

    blank(first, (0, TILE))

    def step(source, write, starts):
        def one(index, carry):
            m, side = lax.div(index, 2), lax.rem(index, 2)
            for start in starts:
                advance_tile(
                    loader_side(source, m, side, start),
                    levels,
                    halves,
                    functools.partial(write, m, side, start),
                )
            return carry

        lax.fori_loop(0, members * 2, one, 0)

    def write_second(m, side, start, f, l, h, value):
        second[m, f, l, side, h, pl.ds(start, TILE), :] = value

    step(first, write_second, (REACH, REACH + 4))
    blank(second, (0, TILE))

    row = lax.broadcasted_iota(jnp.int32, (TILE, LANES), 0)

    def write_early(m, side, start, f, l, h, value):
        low = jnp.logical_and(jnp.logical_and(side == 0, outside[0]), row < 4)
        high = jnp.logical_and(jnp.logical_and(side == 1, outside[1]), row >= 4)
        early[m, f, l, side, h] = jnp.where(jnp.logical_or(low, high), 0.0, value)

    step(second, write_early, (2 * REACH,))


def loader_side(ref, m, side, start):
    def load(f, l, h, shift):
        return ref[m, f, l, side, h, pl.ds(start + shift, TILE), :]

    return load


def late_edge_kernel(dims, early, kept, late, pert_low, pert_high, pair, cross, sums, done, fields, total, first, second, third, sems):
    members, levels, rows, halves, total_rows = dims
    tile = lax.axis_index("tile")
    last_tile = lax.axis_size("tile") - 1
    odd = lax.rem(tile, 2) == 1
    outside = (tile == 0, tile == last_tile)
    row = lax.broadcasted_iota(jnp.int32, (TILE, LANES), 0)

    def fill(m, carry):
        for f in range(4):
            for l in range(levels):
                for h in range(halves):
                    cols = slice(h * LANES, (h + 1) * LANES)
                    from_pair = pair[m, f, l, :, cols]
                    from_cross = cross[m, f, l, :, cols]
                    below = jnp.where(odd, from_pair, from_cross)
                    above = jnp.where(odd, from_cross, from_pair)
                    below = jnp.where(outside[0], 0.0, below)
                    above = jnp.where(outside[1], 0.0, above)
                    first[m, f, l, 0, h, 4:8, :] = early[m, f, l, 0, h, 0:4, :] + below
                    first[m, f, l, 0, h, 8:12, :] = early[m, f, l, 0, h, 4:8, :] + pert_low[m, f, l, 0:4, cols]
                    first[m, f, l, 0, h, 12:20, :] = kept[m, f, l, 0, h]
                    first[m, f, l, 1, h, 4:12, :] = kept[m, f, l, 1, h]
                    first[m, f, l, 1, h, 12:16, :] = early[m, f, l, 1, h, 0:4, :] + pert_high[m, f, l, 4:8, cols]
                    first[m, f, l, 1, h, 16:20, :] = early[m, f, l, 1, h, 4:8, :] + above
                    second[m, f, l, 0, h, 14:22, :] = late[m, f, l, 0, h]
                    second[m, f, l, 1, h, 2:10, :] = late[m, f, l, 1, h]
        return carry

    lax.fori_loop(0, members, fill, 0)

    def third_step(m, carry):
        for side, start in ((0, 6), (1, 10)):
            beyond = jnp.logical_and(outside[side], (row < 2) if side == 0 else (row >= 6))

            def store(f, l, h, value):
                second[m, f, l, side, h, start : start + TILE, :] = jnp.where(beyond, 0.0, value)

            advance_tile(loader_side(first, m, side, start), levels, halves, store)
        return carry

    lax.fori_loop(0, members, third_step, 0)

    def copy(m, side, h):
        return pltpu.make_async_copy(
            third.at[m, :, :, side, h],
            fields.at[m, :, :, pl.ds(side * (rows - TILE), TILE), half(h)],
            sems.at[m, side, h],
        )

    def fourth_step(m, carry):
        acc = sums[m]
        for side in range(2):
            squares = []

            def store(f, l, h, value):
                third[m, f, l, side, h] = value
                if f == 2:
                    squares.append(value * value)

            advance_tile(loader_side(second, m, side, 8), levels, halves, store)
            acc += latitude(tile * rows + side * (rows - TILE), total_rows) * sum(squares)
            for h in range(halves):
                copy(m, side, h).start()
        total[m] = jnp.full((TILE, LANES), jnp.sum(acc) / (levels * total_rows * halves * LANES), jnp.float32)
        return carry

    lax.fori_loop(0, members, fourth_step, 0)
    for m in range(members):
        for side in range(2):
            for h in range(halves):
                copy(m, side, h).wait()


def tile_sum(value, count):
    if count & (count - 1):
        return lax.psum(value, "tile")
    reach = 1
    while reach < count:
        value = value + lax.ppermute(value, "tile", [(i, i ^ reach) for i in range(count)])
        reach *= 2
    return value


def body(state, perturbation, ancestors):
    members, fields_n, levels, rows, columns = state.shape
    halves = columns // LANES
    count = lax.axis_size("tile")
    tile = lax.axis_index("tile")
    total_rows = rows * count
    dims = (members, levels, rows, halves, total_rows)
    odd = lax.rem(tile, 2) == 1
    pair_pairs = [(i, i ^ 1) for i in range(count)]
    cross_pairs = [(i, i + 1 if i % 2 else i - 1) for i in range(1, count - 1)]

    other = lax.ppermute(state, "member", [(0, 1), (1, 0)])

    def edge(array, width, low):
        start = jnp.where(low, 0, rows - width)
        return lax.dynamic_slice_in_dim(array, start, width, axis=3)

    pair = lax.ppermute(edge(state, DEEP, odd), "tile", pair_pairs)
    cross = lax.ppermute(edge(state, DEEP, ~odd), "tile", cross_pairs)
    pert_pair = lax.ppermute(edge(perturbation, SHALLOW, odd), "tile", pair_pairs)
    pert_cross = lax.ppermute(edge(perturbation, SHALLOW, ~odd), "tile", cross_pairs)

    def vmem():
        return pl.BlockSpec(memory_space=pltpu.VMEM)

    def anywhere():
        return pl.BlockSpec(memory_space=pl.ANY)

    def smem():
        return pl.BlockSpec(memory_space=pltpu.SMEM)

    f32 = jnp.float32
    grid = (members, 4, levels, halves, rows + 2 * TILE, LANES)
    edges = (members, 4, levels, 2, halves, TILE, LANES)
    cells = members * 4 * levels * rows * columns
    done, sums, kept, late = pl.pallas_call(
        functools.partial(interior_kernel, dims),
        out_shape=(
            jax.ShapeDtypeStruct(state.shape, f32),
            jax.ShapeDtypeStruct((members, TILE, LANES), f32),
            jax.ShapeDtypeStruct(edges, f32),
            jax.ShapeDtypeStruct(edges, f32),
        ),
        in_specs=[smem(), anywhere(), anywhere(), anywhere()],
        out_specs=(anywhere(), vmem(), vmem(), vmem()),
        scratch_shapes=[
            pltpu.VMEM(grid, f32),
            pltpu.VMEM(grid, f32),
            pltpu.VMEM(grid, f32),
            pltpu.SemaphoreType.DMA((3 * members, halves)),
        ],
        compiler_params=pltpu.CompilerParams(vmem_limit_bytes=24 * 1024 * 1024),
        cost_estimate=pl.CostEstimate(flops=cells * 100, bytes_accessed=cells * 16, transcendentals=cells),
        name="interior",
    )(ancestors, state, other, perturbation)

    other_pair = lax.ppermute(pair, "member", [(0, 1), (1, 0)])
    other_cross = lax.ppermute(cross, "member", [(0, 1), (1, 0)])
    early = pl.pallas_call(
        functools.partial(early_edge_kernel, dims),
        out_shape=jax.ShapeDtypeStruct(edges, f32),
        in_specs=[smem()] + [anywhere()] * 6,
        out_specs=vmem(),
        scratch_shapes=[
            pltpu.VMEM((members, 4, levels, 2, halves, BAND, LANES), f32),
            pltpu.VMEM((members, 4, levels, 2, halves, BAND, LANES), f32),
            pltpu.SemaphoreType.DMA((members, 2, 2, halves)),
        ],
        compiler_params=pltpu.CompilerParams(vmem_limit_bytes=16 * 1024 * 1024),
        cost_estimate=pl.CostEstimate(flops=cells * 20, bytes_accessed=cells * 4, transcendentals=cells),
        name="early_edge",
    )(ancestors, state, other, pair, cross, other_pair, other_cross)

    pert_low = perturbation[:, :, :, :TILE]
    pert_high = perturbation[:, :, :, rows - TILE :]
    evolved, total = pl.pallas_call(
        functools.partial(late_edge_kernel, dims),
        out_shape=(
            jax.ShapeDtypeStruct(state.shape, f32),
            jax.ShapeDtypeStruct((members, TILE, LANES), f32),
        ),
        in_specs=[vmem()] * 8 + [anywhere()],
        out_specs=(anywhere(), vmem()),
        scratch_shapes=[
            pltpu.VMEM((members, 4, levels, 2, halves, STRIP, LANES), f32),
            pltpu.VMEM((members, 4, levels, 2, halves, STRIP, LANES), f32),
            pltpu.VMEM(edges, f32),
            pltpu.SemaphoreType.DMA((members, 2, halves)),
        ],
        input_output_aliases={8: 0},
        compiler_params=pltpu.CompilerParams(vmem_limit_bytes=24 * 1024 * 1024),
        cost_estimate=pl.CostEstimate(flops=cells * 20, bytes_accessed=cells * 4, transcendentals=cells),
        name="late_edge",
    )(early, kept, late, pert_low, pert_high, pert_pair, pert_cross, sums, done)

    observable = tile_sum(total, count)[:, 0, 0]
    return evolved, observable


def solution(mesh):
    return jax.shard_map(
        body,
        mesh=mesh,
        in_specs=(
            P(("groups", "member"), None, None, "tile", None),
            P(("groups", "member"), None, None, "tile", None),
            P("groups"),
        ),
        out_specs=(P(("groups", "member"), None, None, "tile", None), P(("groups", "member"))),
        check_vma=False,
    )
```

```python
import functools

import jax
import jax.numpy as jnp
from jax import lax
from jax.experimental import pallas as pl
from jax.experimental.pallas import tpu as pltpu
from jax.sharding import PartitionSpec as P

STEPS_EACH = 2
TIME_STEP = 0.15
DIFFUSION = 0.2
MIXING = 0.1
CORIOLIS = 0.5
BUOYANCY_GAIN = 0.3
STRATIFICATION = 0.3
SATURATION = 0.5
LATENT = 0.5

LANES = 128
TILE = 8
REACH = 2
SHALLOW = 2 * REACH

INTERIOR_LIMIT = 16 * 1024 * 1024
RIM_LIMIT = 16 * 1024 * 1024

KEEP = 1.0 - TIME_STEP * (4.0 * DIFFUSION + 2.0 * MIXING)
SPREAD = TIME_STEP * DIFFUSION
LIFT = TIME_STEP * MIXING
NEAR = TIME_STEP * 8.0 / 12.0
FAR = TIME_STEP / 12.0


def shifted(parts, by):
    lane = lax.broadcasted_iota(jnp.int32, parts[0].shape, 1)
    turned = [pltpu.roll(part, (-by) % LANES, 1) for part in parts]
    count = len(parts)
    if by > 0:
        return [jnp.where(lane >= LANES - by, turned[(h + 1) % count], turned[h]) for h in range(count)]
    return [jnp.where(lane < -by, turned[(h - 1) % count], turned[h]) for h in range(count)]


def advance_tile(load, levels, halves, store):
    for l in range(levels):
        up, down = min(l + 1, levels - 1), max(l - 1, 0)
        centre = [[load(f, l, h, 0) for h in range(halves)] for f in range(4)]
        winds = []
        for h in range(halves):
            e, n = centre[0][h], centre[1][h]
            en, nn = NEAR * e, NEAR * n
            winds.append((SPREAD - en, SPREAD + en, FAR * e, SPREAD - nn, SPREAD + nn, FAR * n))
        updated = []
        for f in range(4):
            c = centre[f]
            e1, w1, e2, w2 = shifted(c, 1), shifted(c, -1), shifted(c, 2), shifted(c, -2)
            row = []
            for h in range(halves):
                ae, aw, ax, an, as_, ay = winds[h]
                new = KEEP * c[h] + LIFT * (load(f, up, h, 0) + load(f, down, h, 0))
                new += ae * e1[h] + aw * w1[h] + ax * (e2[h] - w2[h])
                new += an * load(f, l, h, 1) + as_ * load(f, l, h, -1)
                new += ay * (load(f, l, h, 2) - load(f, l, h, -2))
                row.append(new)
            updated.append(row)
        for h in range(halves):
            e, n, b = centre[0][h], centre[1][h], centre[2][h]
            turn = (TIME_STEP * CORIOLIS) * n
            store(0, l, h, updated[0][h] + turn)
            store(1, l, h, updated[1][h] - (TIME_STEP * CORIOLIS) * e + (TIME_STEP * BUOYANCY_GAIN) * b)
            b_new = updated[2][h] - (TIME_STEP * STRATIFICATION) * n
            q_new = updated[3][h]
            excess = jnp.maximum(q_new - SATURATION * jnp.exp(0.1 * b_new), 0.0)
            store(2, l, h, b_new + LATENT * excess)
            store(3, l, h, q_new - excess)


def loader(ref, m, start):
    def load(f, l, h, shift):
        return ref[m, f, l, h, pl.ds(start + shift, TILE), :]

    return load


def latitude(first_row, total_rows):
    rows = first_row + lax.broadcasted_iota(jnp.int32, (TILE, LANES), 0)
    return 1.0 + (2.0 / (total_rows - 1)) * rows.astype(jnp.float32)


def half(h):
    return pl.ds(h * LANES, LANES)


def from_source(ancestors, members, slot, own, other, act):
    owner = lax.axis_index("member")
    source = ancestors[owner * members + slot]
    here = lax.div(source, members) == owner
    number = lax.rem(source, members)

    @pl.when(here)
    def _():
        act(own, number)

    @pl.when(jnp.logical_not(here))
    def _():
        act(other, number)


def interior_kernel(dims, ancestors, own, other, pert, sums, zero, one, two, three, noise, sems):
    members, levels, rows, halves, total_rows = dims
    tile = lax.axis_index("tile")

    def state_copies(m, source, number):
        return [
            pltpu.make_async_copy(
                source.at[number, :, :, :, half(h)], zero.at[m, :, :, h, pl.ds(TILE, rows), :], sems.at[0, m, h]
            )
            for h in range(halves)
        ]

    def pert_copies(m):
        return [
            pltpu.make_async_copy(
                pert.at[m, :, :, :, half(h)], noise.at[m, :, :, h, pl.ds(TILE, rows), :], sems.at[1, m, h]
            )
            for h in range(halves)
        ]

    def begin(m, source, number):
        for copy in state_copies(m, source, number):
            copy.start()

    for m in range(members):
        from_source(ancestors, members, m, own, other, functools.partial(begin, m))
    for m in range(members):
        for copy in pert_copies(m):
            copy.start()

    def sweep(source, target, m, start, tiles, post=None):
        for r in range(start, start + tiles * TILE, TILE):

            def store(f, l, h, value):
                if post is not None:
                    value = post(f, l, h, r, value)
                target[m, f, l, h, pl.ds(r, TILE), :] = value

            advance_tile(loader(source, m, r), levels, halves, store)

    for m in range(members):
        for copy in state_copies(m, own, 0):
            copy.wait()
        sweep(zero, one, m, TILE + REACH, rows // TILE)
        for copy in pert_copies(m):
            copy.wait()

        def perturbed(f, l, h, r, value):
            return value + noise[m, f, l, h, pl.ds(r, TILE), :]

        sweep(one, two, m, TILE + 2 * REACH, rows // TILE - 1, perturbed)
        sweep(two, three, m, TILE + 3 * REACH, rows // TILE - 1)
        parts = []

        def counted(f, l, h, r, value):
            if f == 2:
                parts.append(latitude(tile * rows + r - TILE, total_rows) * (value * value))
            return value

        sweep(three, zero, m, 2 * TILE, rows // TILE - 2, counted)
        sums[m] = sum(parts)


def surround(dims, buffer, m, width, near, far):
    members, levels, rows, halves, total_rows = dims
    tile = lax.axis_index("tile")
    odd = lax.rem(tile, 2) == 1
    first, last = tile == 0, tile == lax.axis_size("tile") - 1
    end = TILE + rows
    for f in range(4):
        for l in range(levels):
            for h in range(halves):
                index = (f, l, slice(None), half(h))
                a, b = near(index), far(index)
                buffer[m, f, l, h, TILE - width : TILE, :] = jnp.where(first, 0.0, jnp.where(odd, a, b))
                buffer[m, f, l, h, end : end + width, :] = jnp.where(last, 0.0, jnp.where(odd, b, a))


def pert_rows_kernel(dims, pair, cross, held, noise):
    for m in range(dims[0]):
        surround(dims, noise, m, SHALLOW, lambda index: pair[(m, *index)], lambda index: cross[(m, *index)])


def rim_kernel(
    dims, ancestors, pair, cross, other_pair, other_cross, sums, zero, one, two, three, noise, fields, total, *rest
):
    zero, one, two, three, noise, sems = rest
    members, levels, rows, halves, total_rows = dims
    tile = lax.axis_index("tile")
    outside = (tile == 0, tile == lax.axis_size("tile") - 1)
    end = TILE + rows

    def result_copies(part, start, size):
        return [
            pltpu.make_async_copy(
                zero.at[m, :, :, h, pl.ds(start, size), :],
                fields.at[m, :, :, pl.ds(start - TILE, size), half(h)],
                sems.at[part, m, h],
            )
            for m in range(members)
            for h in range(halves)
        ]

    middle = result_copies(0, 2 * TILE, rows - 2 * TILE)
    for copy in middle:
        copy.start()

    owner = lax.axis_index("member")
    for m in range(members):
        source = ancestors[owner * members + m]
        here = lax.div(source, members) == owner
        number = lax.rem(source, members)

        def chosen(own, other):
            return lambda index: jnp.where(here, own[(number, *index)], other[(number, *index)])

        surround(dims, zero, m, TILE, chosen(pair, other_pair), chosen(cross, other_cross))

    row = lax.broadcasted_iota(jnp.int32, (TILE, LANES), 0)

    def rim_step(source, target, shift, post=None):
        for m in range(members):
            for side, start in enumerate((shift, end - shift)):
                inner = TILE - shift
                beyond = jnp.logical_and(outside[side], row < inner if side == 0 else row >= TILE - inner)

                def store(f, l, h, value):
                    if post is not None:
                        value = post(m, f, l, h, start, value)
                    if inner:
                        value = jnp.where(beyond, 0.0, value)
                    target[m, f, l, h, pl.ds(start, TILE), :] = value

                advance_tile(loader(source, m, start), levels, halves, store)

    def perturbed(m, f, l, h, start, value):
        return value + noise[m, f, l, h, pl.ds(start, TILE), :]

    parts = [[sums[m]] for m in range(members)]

    def counted(m, f, l, h, start, value):
        if f == 2:
            parts[m].append(latitude(tile * rows + start - TILE, total_rows) * (value * value))
        return value

    rim_step(zero, one, REACH)
    rim_step(one, two, 2 * REACH, perturbed)
    rim_step(two, three, 3 * REACH)
    rim_step(three, zero, TILE, counted)
    rims = result_copies(1, TILE, TILE) + result_copies(2, end - TILE, TILE)
    for copy in rims:
        copy.start()
    for m in range(members):
        share = jnp.sum(sum(parts[m])) / (levels * total_rows * halves * LANES)
        total[m] = jnp.full((TILE, LANES), share, jnp.float32)
    for copy in middle + rims:
        copy.wait()


def tile_sum(value, count):
    if count & (count - 1):
        return lax.psum(value, "tile")
    reach = 1
    while reach < count:
        value = value + lax.ppermute(value, "tile", [(i, i ^ reach) for i in range(count)])
        reach *= 2
    return value


def body(state, perturbation, ancestors):
    members, _, levels, rows, columns = state.shape
    halves = columns // LANES
    count, groups = lax.axis_size("tile"), lax.axis_size("groups")
    dims = (members, levels, rows, halves, rows * count)
    odd = lax.rem(lax.axis_index("tile"), 2) == 1
    f32 = jnp.float32

    def to_pair(array):
        return lax.ppermute(array, "tile", [(i, i ^ 1) for i in range(count)])

    def to_cross(array):
        def partner(group, i):
            if i in (0, count - 1):
                return (group ^ 1) * count + i if groups % 2 == 0 else group * count + count - 1 - i
            return group * count + (i + 1 if i % 2 else i - 1)

        pairs = [(group * count + i, partner(group, i)) for group in range(groups) for i in range(count)]
        return lax.ppermute(array, ("groups", "tile"), pairs)

    def edge(array, width, low):
        return lax.dynamic_slice_in_dim(array, jnp.where(low, 0, rows - width), width, axis=3)

    def to_member(array):
        return lax.ppermute(array, "member", [(0, 1), (1, 0)])

    def spec(space):
        return pl.BlockSpec(memory_space=space)

    other = to_member(state)
    pair, cross = to_pair(edge(state, TILE, odd)), to_cross(edge(state, TILE, ~odd))
    near, far = edge(perturbation, SHALLOW, odd), edge(perturbation, SHALLOW, ~odd)
    ancestors, near, far = lax.optimization_barrier((ancestors, near, far))
    pert_pair, pert_cross = to_pair(near), to_cross(far)

    cells = state.size
    buffer = jax.ShapeDtypeStruct((members, 4, levels, halves, rows + 2 * TILE, LANES), f32)
    sums_shape = jax.ShapeDtypeStruct((members, TILE, LANES), f32)
    sums, *buffers = pl.pallas_call(
        functools.partial(interior_kernel, dims),
        out_shape=(sums_shape,) + (buffer,) * 5,
        in_specs=[spec(pltpu.SMEM), spec(pl.ANY), spec(pl.ANY), spec(pl.ANY)],
        out_specs=(spec(pltpu.VMEM),) * 6,
        scratch_shapes=[pltpu.SemaphoreType.DMA((2, members, halves))],
        compiler_params=pltpu.CompilerParams(vmem_limit_bytes=INTERIOR_LIMIT),
        cost_estimate=pl.CostEstimate(flops=cells * 100, bytes_accessed=cells * 16, transcendentals=cells),
        name="interior",
    )(ancestors, state, other, perturbation)

    pair, cross, pert_pair, pert_cross, sums = lax.optimization_barrier((pair, cross, pert_pair, pert_cross, sums))
    other_pair, other_cross = to_member(pair), to_member(cross)
    buffers[4] = pl.pallas_call(
        functools.partial(pert_rows_kernel, dims),
        out_shape=buffer,
        in_specs=[spec(pltpu.VMEM)] * 3,
        out_specs=spec(pltpu.VMEM),
        input_output_aliases={2: 0},
        compiler_params=pltpu.CompilerParams(vmem_limit_bytes=RIM_LIMIT),
        cost_estimate=pl.CostEstimate(flops=0, bytes_accessed=cells * 100, transcendentals=0),
        name="pert_rows",
    )(pert_pair, pert_cross, buffers[4])
    evolved, total, *_ = pl.pallas_call(
        functools.partial(rim_kernel, dims),
        out_shape=(jax.ShapeDtypeStruct(state.shape, f32), sums_shape) + (buffer,) * 5,
        in_specs=[spec(pltpu.SMEM)] + [spec(pltpu.VMEM)] * 10,
        out_specs=(spec(pl.ANY),) + (spec(pltpu.VMEM),) * 6,
        scratch_shapes=[pltpu.SemaphoreType.DMA((3, members, halves))],
        input_output_aliases={6: 2, 7: 3, 8: 4, 9: 5, 10: 6},
        compiler_params=pltpu.CompilerParams(vmem_limit_bytes=RIM_LIMIT),
        cost_estimate=pl.CostEstimate(flops=cells * 30, bytes_accessed=cells * 8, transcendentals=cells),
        name="rim",
    )(ancestors, pair, cross, other_pair, other_cross, sums, *buffers)

    observable = tile_sum(total, count)[:, 0, 0]
    return evolved, observable


def solution(mesh):
    return jax.shard_map(
        body,
        mesh=mesh,
        in_specs=(
            P(("groups", "member"), None, None, "tile", None),
            P(("groups", "member"), None, None, "tile", None),
            P("groups"),
        ),
        out_specs=(P(("groups", "member"), None, None, "tile", None), P(("groups", "member"))),
        check_vma=False,
    )
```

```python
import functools

import jax
import jax.numpy as jnp
from jax import lax
from jax.experimental import pallas as pl
from jax.experimental.pallas import tpu as pltpu
from jax.sharding import PartitionSpec as P

STEPS_EACH = 2
TIME_STEP = 0.15
DIFFUSION = 0.2
MIXING = 0.1
CORIOLIS = 0.5
BUOYANCY_GAIN = 0.3
STRATIFICATION = 0.3
SATURATION = 0.5
LATENT = 0.5

LANES = 128
TILE = 8
REACH = 2
WIDTH = 2 * REACH

VMEM_LIMIT = 16 * 1024 * 1024
WIDE_LIMIT = 16 * 1024 * 1024

KEEP = 1.0 - TIME_STEP * (4.0 * DIFFUSION + 2.0 * MIXING)
SPREAD = TIME_STEP * DIFFUSION
LIFT = TIME_STEP * MIXING
NEAR = TIME_STEP * 8.0 / 12.0
FAR = TIME_STEP / 12.0


def shifted(parts, by):
    lane = lax.broadcasted_iota(jnp.int32, parts[0].shape, 1)
    turned = [pltpu.roll(part, (-by) % LANES, 1) for part in parts]
    count = len(parts)
    if by > 0:
        return [jnp.where(lane >= LANES - by, turned[(h + 1) % count], turned[h]) for h in range(count)]
    return [jnp.where(lane < -by, turned[(h - 1) % count], turned[h]) for h in range(count)]


def advance_tile(load, levels, halves, store):
    for l in range(levels):
        up, down = min(l + 1, levels - 1), max(l - 1, 0)
        centre = [[load(f, l, h, 0) for h in range(halves)] for f in range(4)]
        winds = []
        for h in range(halves):
            e, n = centre[0][h], centre[1][h]
            en, nn = NEAR * e, NEAR * n
            winds.append((SPREAD - en, SPREAD + en, FAR * e, SPREAD - nn, SPREAD + nn, FAR * n))
        updated = []
        for f in range(4):
            c = centre[f]
            e1, w1, e2, w2 = shifted(c, 1), shifted(c, -1), shifted(c, 2), shifted(c, -2)
            row = []
            for h in range(halves):
                ae, aw, ax, an, as_, ay = winds[h]
                new = KEEP * c[h] + LIFT * (load(f, up, h, 0) + load(f, down, h, 0))
                new += ae * e1[h] + aw * w1[h] + ax * (e2[h] - w2[h])
                new += an * load(f, l, h, 1) + as_ * load(f, l, h, -1)
                new += ay * (load(f, l, h, 2) - load(f, l, h, -2))
                row.append(new)
            updated.append(row)
        for h in range(halves):
            e, n, b = centre[0][h], centre[1][h], centre[2][h]
            turn = (TIME_STEP * CORIOLIS) * n
            store(0, l, h, updated[0][h] + turn)
            store(1, l, h, updated[1][h] - (TIME_STEP * CORIOLIS) * e + (TIME_STEP * BUOYANCY_GAIN) * b)
            b_new = updated[2][h] - (TIME_STEP * STRATIFICATION) * n
            q_new = updated[3][h]
            excess = jnp.maximum(q_new - SATURATION * jnp.exp(0.1 * b_new), 0.0)
            store(2, l, h, b_new + LATENT * excess)
            store(3, l, h, q_new - excess)


def loader(ref, m, start):
    def load(f, l, h, shift):
        return ref[m, f, l, h, pl.ds(start + shift, TILE), :]

    return load


def latitude(first_row, total_rows):
    rows = first_row + lax.broadcasted_iota(jnp.int32, (TILE, LANES), 0)
    return 1.0 + (2.0 / (total_rows - 1)) * rows.astype(jnp.float32)


def half(h):
    return pl.ds(h * LANES, LANES)


def from_source(ancestors, members, slot, own, other, act):
    owner = lax.axis_index("member")
    source = ancestors[owner * members + slot]
    here = lax.div(source, members) == owner
    number = lax.rem(source, members)

    @pl.when(here)
    def _():
        act(own, number)

    @pl.when(jnp.logical_not(here))
    def _():
        act(other, number)


def sweep(dims, source, target, m, starts, post=None):
    members, levels, rows, halves, total_rows = dims
    for start in starts:

        def store(f, l, h, value):
            if post is not None:
                value = post(f, l, h, start, value)
            target[m, f, l, h, pl.ds(start, TILE), :] = value

        advance_tile(loader(source, m, start), levels, halves, store)


def inner_starts(rows):
    first = range(2 * TILE - REACH, rows + REACH, TILE)
    second = range(2 * TILE, rows, TILE)
    return first, second


def perturbed(noise, m):
    def post(f, l, h, start, value):
        return value + noise[m, f, l, h, pl.ds(start, TILE), :]

    return post


def weighed(dims, parts):
    members, levels, rows, halves, total_rows = dims
    offset = lax.axis_index("tile") * rows - TILE

    def post(f, l, h, start, value):
        if f == 2:
            parts.append(latitude(offset + start, total_rows) * (value * value))
        return value

    return post


def split_edges(dims, low, high, to_pair, to_cross):
    members, levels, rows, halves, total_rows = dims
    odd = lax.rem(lax.axis_index("tile"), 2) == 1
    for m in range(members):
        for f in range(4):
            for l in range(levels):
                for h in range(halves):
                    a, b = low(m, f, l, h), high(m, f, l, h)
                    to_pair[m, f, l, :, half(h)] = jnp.where(odd, a, b)
                    to_cross[m, f, l, :, half(h)] = jnp.where(odd, b, a)


def edge_kernel(dims, low, high, to_pair, to_cross):
    split_edges(
        dims, lambda m, f, l, h: low[m, f, l, :, half(h)], lambda m, f, l, h: high[m, f, l, :, half(h)], to_pair, to_cross
    )


def inner_early_kernel(dims, ancestors_in, own, other, pert, mark, zero, one, two, noise, ancestors, sems, sem):
    members, levels, rows, halves, total_rows = dims
    first, second = inner_starts(rows)
    owner = lax.axis_index("member")

    def copies(source, number, target, part, m):
        return [
            pltpu.make_async_copy(
                source.at[number, :, :, :, half(h)], target.at[m, :, :, h, pl.ds(TILE, rows), :], sems.at[part, m, h]
            )
            for h in range(halves)
        ]

    def begin(source, number, m):
        for copy in copies(source, number, zero, 0, m):
            copy.start()

    bring = pltpu.make_async_copy(ancestors_in, ancestors, sem)
    bring.start()
    bring.wait()
    for m in range(members):
        source = ancestors[owner * members + m]
        here = lax.div(source, members) == owner
        number = lax.rem(source, members)
        mark[m] = jnp.full((TILE, LANES), jnp.where(here, number, number + members), jnp.int32)
        pl.when(here)(functools.partial(begin, own, number, m))
        pl.when(jnp.logical_not(here))(functools.partial(begin, other, number, m))
    for m in range(members):
        for copy in copies(pert, m, noise, 1, m):
            copy.start()
    for m in range(members):
        for copy in copies(own, 0, zero, 0, m):
            copy.wait()
        sweep(dims, zero, one, m, first)
        for copy in copies(pert, m, noise, 1, m):
            copy.wait()
        sweep(dims, one, two, m, second, perturbed(noise, m))


def inner_late_kernel(dims, two, sums, three, zero):
    members, levels, rows, halves, total_rows = dims
    first, second = inner_starts(rows)
    for m in range(members):
        parts = []
        sweep(dims, two, three, m, first)
        sweep(dims, three, zero, m, second, weighed(dims, parts))
        sums[m] = sum(parts)


def surround(dims, buffer, m, near, far):
    members, levels, rows, halves, total_rows = dims
    tile = lax.axis_index("tile")
    odd = lax.rem(tile, 2) == 1
    first, last = tile == 0, tile == lax.axis_size("tile") - 1
    end = TILE + rows
    for f in range(4):
        for l in range(levels):
            for h in range(halves):
                index = (f, l, slice(None), half(h))
                a, b = near(index), far(index)
                buffer[m, f, l, h, TILE - WIDTH : TILE, :] = jnp.where(first, 0.0, jnp.where(odd, a, b))
                buffer[m, f, l, h, end : end + WIDTH, :] = jnp.where(last, 0.0, jnp.where(odd, b, a))


def outer_step(dims, source, target, m):
    members, levels, rows, halves, total_rows = dims
    tile = lax.axis_index("tile")
    row = lax.broadcasted_iota(jnp.int32, (TILE, LANES), 0)
    below = jnp.logical_and(tile == 0, row < REACH)
    above = jnp.logical_and(tile == lax.axis_size("tile") - 1, row >= TILE - REACH)
    for start, beyond in ((TILE - REACH, below), (rows + REACH, above)):
        sweep(dims, source, target, m, (start,), lambda f, l, h, start, value: jnp.where(beyond, 0.0, value))


def outer_early_kernel(dims, pair, cross, other_pair, other_cross, mark, noise, zero_in, one_in, two_in,
                       to_pair, to_cross, zero, one, two):
    members, levels, rows, halves, total_rows = dims
    for m in range(members):
        place = mark[m, :WIDTH, :]

        def chosen(own, other):
            def read(index):
                value = own[(0, *index)]
                for k in range(1, 2 * members):
                    array = own if k < members else other
                    value = jnp.where(place == k, array[(k % members, *index)], value)
                return value

            return read

        surround(dims, zero, m, chosen(pair, other_pair), chosen(cross, other_cross))
        outer_step(dims, zero, one, m)
        sweep(dims, one, two, m, (TILE, rows), perturbed(noise, m))
    split_edges(
        dims,
        lambda m, f, l, h: two[m, f, l, h, TILE : TILE + WIDTH, :],
        lambda m, f, l, h: two[m, f, l, h, TILE + rows - WIDTH : TILE + rows, :],
        to_pair,
        to_cross,
    )


def outer_late_kernel(dims, pair, cross, sums, two_in, three_in, zero_in, fields, total, two, three, zero, sems):
    members, levels, rows, halves, total_rows = dims

    def copies(part, m, start, size):
        return [
            pltpu.make_async_copy(
                zero.at[m, :, :, h, pl.ds(start, size), :],
                fields.at[m, :, :, pl.ds(start - TILE, size), half(h)],
                sems.at[part, m, h],
            )
            for h in range(halves)
        ]

    started = []
    for m in range(members):
        started += copies(0, m, 2 * TILE, rows - 2 * TILE)
    for copy in started:
        copy.start()
    for m in range(members):
        surround(dims, two, m, lambda index: pair[(m, *index)], lambda index: cross[(m, *index)])
        outer_step(dims, two, three, m)
        parts = [sums[m]]
        for part, start in ((1, TILE), (2, rows)):
            sweep(dims, three, zero, m, (start,), weighed(dims, parts))
            for copy in copies(part, m, start, TILE):
                copy.start()
                started.append(copy)
        total[m] = sum(parts)
    for copy in started:
        copy.wait()


def tile_sum(value, count):
    if count & (count - 1):
        return lax.psum(value, "tile")
    reach = 1
    while reach < count:
        value = value + lax.ppermute(value, "tile", [(i, i ^ reach) for i in range(count)])
        reach *= 2
    return value


def body(state, perturbation, ancestors):
    members, _, levels, rows, columns = state.shape
    halves = columns // LANES
    count, groups = lax.axis_size("tile"), lax.axis_size("groups")
    dims = (members, levels, rows, halves, rows * count)
    f32 = jnp.float32

    def to_pair(array):
        return lax.ppermute(array, "tile", [(i, i ^ 1) for i in range(count)])

    def to_cross(array):
        def partner(group, i):
            if i in (0, count - 1):
                return (group ^ 1) * count + i if groups % 2 == 0 else group * count + count - 1 - i
            return group * count + (i + 1 if i % 2 else i - 1)

        pairs = [(group * count + i, partner(group, i)) for group in range(groups) for i in range(count)]
        return lax.ppermute(array, ("groups", "tile"), pairs)

    def to_member(array):
        return lax.ppermute(array, "member", [(0, 1), (1, 0)])

    def in_hbm(array):
        return pltpu.with_memory_space_constraint(array, pltpu.HBM)

    def spec(space):
        return pl.BlockSpec(memory_space=space)

    vmem, anywhere = spec(pltpu.VMEM), spec(pl.ANY)
    params = pltpu.CompilerParams(vmem_limit_bytes=VMEM_LIMIT)
    cells = state.size

    def cost(part):
        return pl.CostEstimate(flops=cells * part, bytes_accessed=cells * part, transcendentals=0)

    buffer = jax.ShapeDtypeStruct((members, 4, levels, halves, rows + 2 * TILE, LANES), f32)
    tile = jax.ShapeDtypeStruct((members, TILE, LANES), f32)
    strip = jax.ShapeDtypeStruct((members, 4, levels, WIDTH, columns), f32)

    other = to_member(state)
    edge_pair, edge_cross = pl.pallas_call(
        functools.partial(edge_kernel, dims),
        out_shape=(strip, strip),
        in_specs=[vmem, vmem],
        out_specs=(vmem, vmem),
        compiler_params=params,
        cost_estimate=cost(0),
        name="edge",
    )(state[:, :, :, :WIDTH], state[:, :, :, rows - WIDTH :])
    pair, cross = to_pair(edge_pair), to_cross(edge_cross)
    mark, zero, one, two, noise = pl.pallas_call(
        functools.partial(inner_early_kernel, dims),
        out_shape=(jax.ShapeDtypeStruct(tile.shape, jnp.int32),) + (buffer,) * 4,
        in_specs=[anywhere] * 4,
        out_specs=(vmem,) * 5,
        scratch_shapes=[
            pltpu.SMEM(ancestors.shape, jnp.int32),
            pltpu.SemaphoreType.DMA((2, members, halves)),
            pltpu.SemaphoreType.DMA,
        ],
        compiler_params=pltpu.CompilerParams(vmem_limit_bytes=WIDE_LIMIT),
        cost_estimate=cost(20),
        name="inner_early",
    )(in_hbm(ancestors), in_hbm(state), other, in_hbm(perturbation))
    pair, cross, mark = lax.optimization_barrier((pair, cross, mark))
    other_pair, other_cross = to_member(pair), to_member(cross)
    edge_pair, edge_cross, zero, one, two = pl.pallas_call(
        functools.partial(outer_early_kernel, dims),
        out_shape=(strip, strip) + (buffer,) * 3,
        in_specs=[vmem] * 9,
        out_specs=(vmem,) * 5,
        input_output_aliases={6: 2, 7: 3, 8: 4},
        compiler_params=params,
        cost_estimate=cost(5),
        name="outer_early",
    )(pair, cross, other_pair, other_cross, mark, noise, zero, one, two)

    pair, cross = to_pair(edge_pair), to_cross(edge_cross)
    sums, three, zero = pl.pallas_call(
        functools.partial(inner_late_kernel, dims),
        out_shape=(tile, buffer, buffer),
        in_specs=[vmem],
        out_specs=(vmem,) * 3,
        compiler_params=params,
        cost_estimate=cost(20),
        name="inner_late",
    )(two)
    pair, cross, sums = lax.optimization_barrier((pair, cross, sums))
    evolved, total, *_ = pl.pallas_call(
        functools.partial(outer_late_kernel, dims),
        out_shape=(jax.ShapeDtypeStruct(state.shape, f32), tile) + (buffer,) * 3,
        in_specs=[vmem] * 6,
        out_specs=(anywhere,) + (vmem,) * 4,
        scratch_shapes=[pltpu.SemaphoreType.DMA((3, members, halves))],
        input_output_aliases={3: 2, 4: 3, 5: 4},
        compiler_params=params,
        cost_estimate=cost(5),
        name="outer_late",
    )(pair, cross, sums, two, three, zero)

    observable = jnp.sum(tile_sum(total, count), axis=(1, 2)) / (levels * rows * count * columns)
    return evolved, observable


def solution(mesh):
    return jax.shard_map(
        body,
        mesh=mesh,
        in_specs=(
            P(("groups", "member"), None, None, "tile", None),
            P(("groups", "member"), None, None, "tile", None),
            P("groups"),
        ),
        out_specs=(P(("groups", "member"), None, None, "tile", None), P(("groups", "member"))),
        check_vma=False,
    )
```

```python
import functools

import jax
import jax.numpy as jnp
from jax import lax
from jax.experimental import pallas as pl
from jax.experimental.pallas import tpu as pltpu
from jax.sharding import PartitionSpec as P

STEPS_EACH = 2
TIME_STEP = 0.15
DIFFUSION = 0.2
MIXING = 0.1
CORIOLIS = 0.5
BUOYANCY_GAIN = 0.3
STRATIFICATION = 0.3
SATURATION = 0.5
LATENT = 0.5

LANES = 128
TILE = 8
REACH = 2
WIDTH = 2 * REACH

VMEM_LIMIT = 16 * 1024 * 1024
WIDE_LIMIT = 16 * 1024 * 1024

KEEP = 1.0 - TIME_STEP * (4.0 * DIFFUSION + 2.0 * MIXING)
SPREAD = TIME_STEP * DIFFUSION
LIFT = TIME_STEP * MIXING
NEAR = TIME_STEP * 8.0 / 12.0
FAR = TIME_STEP / 12.0


def shifted(parts, by):
    lane = lax.broadcasted_iota(jnp.int32, parts[0].shape, 1)
    turned = [pltpu.roll(part, (-by) % LANES, 1) for part in parts]
    count = len(parts)
    if by > 0:
        return [jnp.where(lane >= LANES - by, turned[(h + 1) % count], turned[h]) for h in range(count)]
    return [jnp.where(lane < -by, turned[(h - 1) % count], turned[h]) for h in range(count)]


def advance_tile(load, levels, halves, store):
    for l in range(levels):
        up, down = min(l + 1, levels - 1), max(l - 1, 0)
        centre = [[load(f, l, h, 0) for h in range(halves)] for f in range(4)]
        winds = []
        for h in range(halves):
            e, n = centre[0][h], centre[1][h]
            en, nn = NEAR * e, NEAR * n
            winds.append((SPREAD - en, SPREAD + en, FAR * e, SPREAD - nn, SPREAD + nn, FAR * n))
        updated = []
        for f in range(4):
            c = centre[f]
            e1, w1, e2, w2 = shifted(c, 1), shifted(c, -1), shifted(c, 2), shifted(c, -2)
            row = []
            for h in range(halves):
                ae, aw, ax, an, as_, ay = winds[h]
                new = KEEP * c[h] + LIFT * (load(f, up, h, 0) + load(f, down, h, 0))
                new += ae * e1[h] + aw * w1[h] + ax * (e2[h] - w2[h])
                new += an * load(f, l, h, 1) + as_ * load(f, l, h, -1)
                new += ay * (load(f, l, h, 2) - load(f, l, h, -2))
                row.append(new)
            updated.append(row)
        for h in range(halves):
            e, n, b = centre[0][h], centre[1][h], centre[2][h]
            turn = (TIME_STEP * CORIOLIS) * n
            store(0, l, h, updated[0][h] + turn)
            store(1, l, h, updated[1][h] - (TIME_STEP * CORIOLIS) * e + (TIME_STEP * BUOYANCY_GAIN) * b)
            b_new = updated[2][h] - (TIME_STEP * STRATIFICATION) * n
            q_new = updated[3][h]
            excess = jnp.maximum(q_new - SATURATION * jnp.exp(0.1 * b_new), 0.0)
            store(2, l, h, b_new + LATENT * excess)
            store(3, l, h, q_new - excess)


def loader(ref, m, start):
    def load(f, l, h, shift):
        return ref[m, f, l, h, pl.ds(start + shift, TILE), :]

    return load


def latitude(first_row, total_rows):
    rows = first_row + lax.broadcasted_iota(jnp.int32, (TILE, LANES), 0)
    return 1.0 + (2.0 / (total_rows - 1)) * rows.astype(jnp.float32)


def half(h):
    return pl.ds(h * LANES, LANES)


def from_source(ancestors, members, slot, own, other, act):
    owner = lax.axis_index("member")
    source = ancestors[owner * members + slot]
    here = lax.div(source, members) == owner
    number = lax.rem(source, members)

    @pl.when(here)
    def _():
        act(own, number)

    @pl.when(jnp.logical_not(here))
    def _():
        act(other, number)


def sweep(dims, source, target, m, starts, post=None):
    members, levels, rows, halves, total_rows = dims
    for start in starts:

        def store(f, l, h, value):
            if post is not None:
                value = post(f, l, h, start, value)
            target[m, f, l, h, pl.ds(start, TILE), :] = value

        advance_tile(loader(source, m, start), levels, halves, store)


def inner_starts(rows):
    first = range(2 * TILE - REACH, rows + REACH, TILE)
    second = range(2 * TILE, rows, TILE)
    return first, second


def perturbed(noise, m):
    def post(f, l, h, start, value):
        return value + noise[m, f, l, h, pl.ds(start, TILE), :]

    return post


def weighed(dims, parts):
    members, levels, rows, halves, total_rows = dims
    offset = lax.axis_index("tile") * rows - TILE

    def post(f, l, h, start, value):
        if f == 2:
            parts.append(latitude(offset + start, total_rows) * (value * value))
        return value

    return post


def split_edges(dims, low, high, to_pair, to_cross):
    members, levels, rows, halves, total_rows = dims
    odd = lax.rem(lax.axis_index("tile"), 2) == 1
    for m in range(members):
        for f in range(4):
            for l in range(levels):
                for h in range(halves):
                    a, b = low(m, f, l, h), high(m, f, l, h)
                    to_pair[m, f, l, :, half(h)] = jnp.where(odd, a, b)
                    to_cross[m, f, l, :, half(h)] = jnp.where(odd, b, a)


def edge_kernel(dims, low, high, to_pair, to_cross):
    split_edges(
        dims, lambda m, f, l, h: low[m, f, l, :, half(h)], lambda m, f, l, h: high[m, f, l, :, half(h)], to_pair, to_cross
    )


def inner_early_kernel(dims, ancestors_in, own, other, pert, mark, zero, one, two, noise, ancestors, sems, sem):
    members, levels, rows, halves, total_rows = dims
    first, second = inner_starts(rows)
    owner = lax.axis_index("member")

    def copies(source, number, target, part, m):
        return [
            pltpu.make_async_copy(
                source.at[number, :, :, :, half(h)], target.at[m, :, :, h, pl.ds(TILE, rows), :], sems.at[part, m, h]
            )
            for h in range(halves)
        ]

    def begin(source, number, m):
        for copy in copies(source, number, zero, 0, m):
            copy.start()

    bring = pltpu.make_async_copy(ancestors_in, ancestors, sem)
    bring.start()
    bring.wait()
    for m in range(members):
        source = ancestors[owner * members + m]
        here = lax.div(source, members) == owner
        number = lax.rem(source, members)
        mark[m] = jnp.full((TILE, LANES), jnp.where(here, number, number + members), jnp.int32)
        pl.when(here)(functools.partial(begin, own, number, m))
        pl.when(jnp.logical_not(here))(functools.partial(begin, other, number, m))
    for m in range(members):
        for copy in copies(pert, m, noise, 1, m):
            copy.start()
    for m in range(members):
        for copy in copies(own, 0, zero, 0, m):
            copy.wait()
        sweep(dims, zero, one, m, first)
        for copy in copies(pert, m, noise, 1, m):
            copy.wait()
        sweep(dims, one, two, m, second, perturbed(noise, m))


def result_copies(dims, buffer, fields, sems, part, m, start, size):
    members, levels, rows, halves, total_rows = dims
    return [
        pltpu.make_async_copy(
            buffer.at[m, :, :, h, pl.ds(start, size), :],
            fields.at[m, :, :, pl.ds(start - TILE, size), half(h)],
            sems.at[part, m, h],
        )
        for h in range(halves)
    ]


def inner_late_kernel(dims, two, sums, three, zero, fields, sems):
    members, levels, rows, halves, total_rows = dims
    first, second = inner_starts(rows)
    middle = len(second) // 2
    started = []
    for m in range(members):
        parts = []
        sweep(dims, two, three, m, first)
        for part, starts in enumerate((second[:middle], second[middle:])):
            sweep(dims, three, zero, m, starts, weighed(dims, parts))
            for copy in result_copies(dims, zero, fields, sems, part, m, starts[0], len(starts) * TILE):
                copy.start()
                started.append(copy)
        sums[m] = sum(parts)
    for copy in started:
        copy.wait()


def surround(dims, buffer, m, near, far):
    members, levels, rows, halves, total_rows = dims
    tile = lax.axis_index("tile")
    odd = lax.rem(tile, 2) == 1
    first, last = tile == 0, tile == lax.axis_size("tile") - 1
    end = TILE + rows
    for f in range(4):
        for l in range(levels):
            for h in range(halves):
                index = (f, l, slice(None), half(h))
                a, b = near(index), far(index)
                buffer[m, f, l, h, TILE - WIDTH : TILE, :] = jnp.where(first, 0.0, jnp.where(odd, a, b))
                buffer[m, f, l, h, end : end + WIDTH, :] = jnp.where(last, 0.0, jnp.where(odd, b, a))


def outer_step(dims, source, target, m):
    members, levels, rows, halves, total_rows = dims
    tile = lax.axis_index("tile")
    row = lax.broadcasted_iota(jnp.int32, (TILE, LANES), 0)
    below = jnp.logical_and(tile == 0, row < REACH)
    above = jnp.logical_and(tile == lax.axis_size("tile") - 1, row >= TILE - REACH)
    for start, beyond in ((TILE - REACH, below), (rows + REACH, above)):
        sweep(dims, source, target, m, (start,), lambda f, l, h, start, value: jnp.where(beyond, 0.0, value))


def outer_early_kernel(dims, pair, cross, other_pair, other_cross, mark, noise, zero_in, one_in, two_in,
                       to_pair, to_cross, zero, one, two):
    members, levels, rows, halves, total_rows = dims
    for m in range(members):
        place = mark[m, :WIDTH, :]

        def chosen(own, other):
            def read(index):
                value = own[(0, *index)]
                for k in range(1, 2 * members):
                    array = own if k < members else other
                    value = jnp.where(place == k, array[(k % members, *index)], value)
                return value

            return read

        surround(dims, zero, m, chosen(pair, other_pair), chosen(cross, other_cross))
        outer_step(dims, zero, one, m)
        sweep(dims, one, two, m, (TILE, rows), perturbed(noise, m))
    split_edges(
        dims,
        lambda m, f, l, h: two[m, f, l, h, TILE : TILE + WIDTH, :],
        lambda m, f, l, h: two[m, f, l, h, TILE + rows - WIDTH : TILE + rows, :],
        to_pair,
        to_cross,
    )


def outer_late_kernel(dims, pair, cross, sums, two_in, three_in, zero_in, total, two, three, zero):
    members, levels, rows, halves, total_rows = dims
    sublane = lax.broadcasted_iota(jnp.int32, (TILE, LANES), 0)
    held = jnp.zeros((TILE, LANES), jnp.float32)
    for m in range(members):
        surround(dims, two, m, lambda index: pair[(m, *index)], lambda index: cross[(m, *index)])
    for m in range(members):
        outer_step(dims, two, three, m)
        parts = [sums[m]]
        sweep(dims, three, zero, m, (TILE, rows), weighed(dims, parts))
        column_sums = jnp.sum(sum(parts), axis=0, keepdims=True) * (1.0 / (levels * total_rows * halves * LANES))
        held = jnp.where(sublane == m, column_sums, held)
    total[...] = held


def place_kernel(dims, zero, inner, fields, sems):
    members, levels, rows, halves, total_rows = dims
    started = []
    for m in range(members):
        for part, start in enumerate((TILE, rows)):
            started += result_copies(dims, zero, fields, sems, part, m, start, TILE)
    for copy in started:
        copy.start()
    for copy in started:
        copy.wait()


def tile_sum(value, count):
    if count & (count - 1):
        return lax.psum(value, "tile")
    reach = 1
    while reach < count:
        value = value + lax.ppermute(value, "tile", [(i, i ^ reach) for i in range(count)])
        reach *= 2
    return value


def body(state, perturbation, ancestors):
    members, _, levels, rows, columns = state.shape
    halves = columns // LANES
    count, groups = lax.axis_size("tile"), lax.axis_size("groups")
    dims = (members, levels, rows, halves, rows * count)
    f32 = jnp.float32

    def to_pair(array):
        return lax.ppermute(array, "tile", [(i, i ^ 1) for i in range(count)])

    def to_cross(array):
        def partner(group, i):
            if i in (0, count - 1):
                return (group ^ 1) * count + i if groups % 2 == 0 else group * count + count - 1 - i
            return group * count + (i + 1 if i % 2 else i - 1)

        pairs = [(group * count + i, partner(group, i)) for group in range(groups) for i in range(count)]
        return lax.ppermute(array, ("groups", "tile"), pairs)

    def to_member(array):
        return lax.ppermute(array, "member", [(0, 1), (1, 0)])

    def in_hbm(array):
        return pltpu.with_memory_space_constraint(array, pltpu.HBM)

    def spec(space):
        return pl.BlockSpec(memory_space=space)

    vmem, anywhere = spec(pltpu.VMEM), spec(pl.ANY)
    params = pltpu.CompilerParams(vmem_limit_bytes=VMEM_LIMIT)
    cells = state.size

    def cost(part):
        return pl.CostEstimate(flops=cells * part, bytes_accessed=cells * part, transcendentals=0)

    buffer = jax.ShapeDtypeStruct((members, 4, levels, halves, rows + 2 * TILE, LANES), f32)
    tile = jax.ShapeDtypeStruct((members, TILE, LANES), f32)
    strip = jax.ShapeDtypeStruct((members, 4, levels, WIDTH, columns), f32)

    other = to_member(state)
    edge_pair, edge_cross = pl.pallas_call(
        functools.partial(edge_kernel, dims),
        out_shape=(strip, strip),
        in_specs=[vmem, vmem],
        out_specs=(vmem, vmem),
        compiler_params=params,
        cost_estimate=cost(0),
        name="edge",
    )(state[:, :, :, :WIDTH], state[:, :, :, rows - WIDTH :])
    pair, cross = to_pair(edge_pair), to_cross(edge_cross)
    mark, zero, one, two, noise = pl.pallas_call(
        functools.partial(inner_early_kernel, dims),
        out_shape=(jax.ShapeDtypeStruct(tile.shape, jnp.int32),) + (buffer,) * 4,
        in_specs=[anywhere] * 4,
        out_specs=(vmem,) * 5,
        scratch_shapes=[
            pltpu.SMEM(ancestors.shape, jnp.int32),
            pltpu.SemaphoreType.DMA((2, members, halves)),
            pltpu.SemaphoreType.DMA,
        ],
        compiler_params=pltpu.CompilerParams(vmem_limit_bytes=WIDE_LIMIT),
        cost_estimate=cost(20),
        name="inner_early",
    )(in_hbm(ancestors), in_hbm(state), other, in_hbm(perturbation))
    pair, cross, mark = lax.optimization_barrier((pair, cross, mark))
    other_pair, other_cross = to_member(pair), to_member(cross)
    edge_pair, edge_cross, zero, one, two = pl.pallas_call(
        functools.partial(outer_early_kernel, dims),
        out_shape=(strip, strip) + (buffer,) * 3,
        in_specs=[vmem] * 9,
        out_specs=(vmem,) * 5,
        input_output_aliases={6: 2, 7: 3, 8: 4},
        compiler_params=params,
        cost_estimate=cost(5),
        name="outer_early",
    )(pair, cross, other_pair, other_cross, mark, noise, zero, one, two)

    pair, cross = to_pair(edge_pair), to_cross(edge_cross)
    result = jax.ShapeDtypeStruct(state.shape, f32)
    sums, three, zero, inner = pl.pallas_call(
        functools.partial(inner_late_kernel, dims),
        out_shape=(tile, buffer, buffer, result),
        in_specs=[vmem],
        out_specs=(vmem,) * 3 + (anywhere,),
        scratch_shapes=[pltpu.SemaphoreType.DMA((2, members, halves))],
        compiler_params=params,
        cost_estimate=cost(20),
        name="inner_late",
    )(two)
    pair, cross, sums = lax.optimization_barrier((pair, cross, sums))
    total, _, _, zero = pl.pallas_call(
        functools.partial(outer_late_kernel, dims),
        out_shape=(jax.ShapeDtypeStruct((TILE, LANES), f32),) + (buffer,) * 3,
        in_specs=[vmem] * 6,
        out_specs=(vmem,) * 4,
        input_output_aliases={3: 1, 4: 2, 5: 3},
        compiler_params=params,
        cost_estimate=cost(5),
        name="outer_late",
    )(pair, cross, sums, two, three, zero)
    evolved = pl.pallas_call(
        functools.partial(place_kernel, dims),
        out_shape=result,
        in_specs=[vmem, anywhere],
        out_specs=anywhere,
        scratch_shapes=[pltpu.SemaphoreType.DMA((2, members, halves))],
        input_output_aliases={1: 0},
        compiler_params=params,
        cost_estimate=cost(5),
        name="place",
    )(zero, inner)
    observable = jnp.sum(tile_sum(total, count), axis=1)[:members]
    return evolved, observable


def solution(mesh):
    return jax.shard_map(
        body,
        mesh=mesh,
        in_specs=(
            P(("groups", "member"), None, None, "tile", None),
            P(("groups", "member"), None, None, "tile", None),
            P("groups"),
        ),
        out_specs=(P(("groups", "member"), None, None, "tile", None), P(("groups", "member"))),
        check_vma=False,
    )
```

```python
import functools

import jax
import jax.numpy as jnp
from jax import lax
from jax.experimental import pallas as pl
from jax.experimental.pallas import tpu as pltpu
from jax.sharding import PartitionSpec as P

STEPS_EACH = 2
TIME_STEP = 0.15
DIFFUSION = 0.2
MIXING = 0.1
CORIOLIS = 0.5
BUOYANCY_GAIN = 0.3
STRATIFICATION = 0.3
SATURATION = 0.5
LATENT = 0.5

LANES = 128
TILE = 8
REACH = 2
WIDTH = 2 * REACH

VMEM_LIMIT = 16 * 1024 * 1024
WIDE_LIMIT = 16 * 1024 * 1024

KEEP = 1.0 - TIME_STEP * (4.0 * DIFFUSION + 2.0 * MIXING)
SPREAD = TIME_STEP * DIFFUSION
LIFT = TIME_STEP * MIXING
NEAR = TIME_STEP * 8.0 / 12.0
FAR = TIME_STEP / 12.0


def shifted(parts, by):
    lane = lax.broadcasted_iota(jnp.int32, parts[0].shape, 1)
    turned = [pltpu.roll(part, (-by) % LANES, 1) for part in parts]
    count = len(parts)
    if by > 0:
        return [jnp.where(lane >= LANES - by, turned[(h + 1) % count], turned[h]) for h in range(count)]
    return [jnp.where(lane < -by, turned[(h - 1) % count], turned[h]) for h in range(count)]


def advance_tile(load, levels, halves, store):
    for l in range(levels):
        up, down = min(l + 1, levels - 1), max(l - 1, 0)
        centre = [[load(f, l, h, 0) for h in range(halves)] for f in range(4)]
        winds = []
        for h in range(halves):
            e, n = centre[0][h], centre[1][h]
            en, nn = NEAR * e, NEAR * n
            winds.append((SPREAD - en, SPREAD + en, FAR * e, SPREAD - nn, SPREAD + nn, FAR * n))
        updated = []
        for f in range(4):
            c = centre[f]
            e1, w1, e2, w2 = shifted(c, 1), shifted(c, -1), shifted(c, 2), shifted(c, -2)
            row = []
            for h in range(halves):
                ae, aw, ax, an, as_, ay = winds[h]
                new = KEEP * c[h] + LIFT * (load(f, up, h, 0) + load(f, down, h, 0))
                new += ae * e1[h] + aw * w1[h] + ax * (e2[h] - w2[h])
                new += an * load(f, l, h, 1) + as_ * load(f, l, h, -1)
                new += ay * (load(f, l, h, 2) - load(f, l, h, -2))
                row.append(new)
            updated.append(row)
        for h in range(halves):
            e, n, b = centre[0][h], centre[1][h], centre[2][h]
            turn = (TIME_STEP * CORIOLIS) * n
            store(0, l, h, updated[0][h] + turn)
            store(1, l, h, updated[1][h] - (TIME_STEP * CORIOLIS) * e + (TIME_STEP * BUOYANCY_GAIN) * b)
            b_new = updated[2][h] - (TIME_STEP * STRATIFICATION) * n
            q_new = updated[3][h]
            excess = jnp.maximum(q_new - SATURATION * jnp.exp(0.1 * b_new), 0.0)
            store(2, l, h, b_new + LATENT * excess)
            store(3, l, h, q_new - excess)


def loader(ref, m, start):
    def load(f, l, h, shift):
        return ref[m, f, l, h, pl.ds(start + shift, TILE), :]

    return load


def latitude(first_row, total_rows):
    rows = first_row + lax.broadcasted_iota(jnp.int32, (TILE, LANES), 0)
    return 1.0 + (2.0 / (total_rows - 1)) * rows.astype(jnp.float32)


def half(h):
    return pl.ds(h * LANES, LANES)


def from_source(ancestors, members, slot, own, other, act):
    owner = lax.axis_index("member")
    source = ancestors[owner * members + slot]
    here = lax.div(source, members) == owner
    number = lax.rem(source, members)

    @pl.when(here)
    def _():
        act(own, number)

    @pl.when(jnp.logical_not(here))
    def _():
        act(other, number)


def sweep(dims, source, target, m, starts, post=None):
    members, levels, rows, halves, total_rows = dims
    for start in starts:

        def store(f, l, h, value):
            if post is not None:
                value = post(f, l, h, start, value)
            target[m, f, l, h, pl.ds(start, TILE), :] = value

        advance_tile(loader(source, m, start), levels, halves, store)


def inner_starts(rows):
    first = range(2 * TILE - REACH, rows + REACH, TILE)
    second = range(2 * TILE, rows, TILE)
    return first, second


def perturbed(noise, m):
    def post(f, l, h, start, value):
        return value + noise[m, f, l, h, pl.ds(start, TILE), :]

    return post


def weighed(dims, parts):
    members, levels, rows, halves, total_rows = dims
    offset = lax.axis_index("tile") * rows - TILE

    def post(f, l, h, start, value):
        if f == 2:
            parts.append(latitude(offset + start, total_rows) * (value * value))
        return value

    return post


def split_edges(dims, low, high, to_pair, to_cross):
    members, levels, rows, halves, total_rows = dims
    odd = lax.rem(lax.axis_index("tile"), 2) == 1
    for m in range(members):
        for f in range(4):
            for l in range(levels):
                for h in range(halves):
                    a, b = low(m, f, l, h), high(m, f, l, h)
                    to_pair[m, f, l, :, half(h)] = jnp.where(odd, a, b)
                    to_cross[m, f, l, :, half(h)] = jnp.where(odd, b, a)


def edge_kernel(dims, low, high, to_pair, to_cross):
    split_edges(
        dims, lambda m, f, l, h: low[m, f, l, :, half(h)], lambda m, f, l, h: high[m, f, l, :, half(h)], to_pair, to_cross
    )


def inner_early_kernel(dims, ancestors_in, own, other, pert, mark, zero, one, two, noise, ancestors, sems, sem):
    members, levels, rows, halves, total_rows = dims
    first, second = inner_starts(rows)
    owner = lax.axis_index("member")

    def copies(source, number, target, part, m):
        return [
            pltpu.make_async_copy(
                source.at[number, :, :, :, half(h)], target.at[m, :, :, h, pl.ds(TILE, rows), :], sems.at[part, m, h]
            )
            for h in range(halves)
        ]

    def begin(source, number, m):
        for copy in copies(source, number, zero, 0, m):
            copy.start()

    bring = pltpu.make_async_copy(ancestors_in, ancestors, sem)
    bring.start()
    bring.wait()
    for m in range(members):
        source = ancestors[owner * members + m]
        here = lax.div(source, members) == owner
        number = lax.rem(source, members)
        mark[m] = jnp.full((TILE, LANES), jnp.where(here, number, number + members), jnp.int32)
        pl.when(here)(functools.partial(begin, own, number, m))
        pl.when(jnp.logical_not(here))(functools.partial(begin, other, number, m))
    for m in range(members):
        for copy in copies(pert, m, noise, 1, m):
            copy.start()
    for m in range(members):
        for copy in copies(own, 0, zero, 0, m):
            copy.wait()
        sweep(dims, zero, one, m, first)
        for copy in copies(pert, m, noise, 1, m):
            copy.wait()
        sweep(dims, one, two, m, second, perturbed(noise, m))


def result_copies(dims, buffer, fields, sems, part, m, start, size):
    members, levels, rows, halves, total_rows = dims
    return [
        pltpu.make_async_copy(
            buffer.at[m, :, :, h, pl.ds(start, size), :],
            fields.at[m, :, :, pl.ds(start - TILE, size), half(h)],
            sems.at[part, m, h],
        )
        for h in range(halves)
    ]


def inner_late_kernel(dims, two, sums, three, zero):
    members, levels, rows, halves, total_rows = dims
    first, second = inner_starts(rows)
    for m in range(members):
        parts = []
        sweep(dims, two, three, m, first)
        sweep(dims, three, zero, m, second, weighed(dims, parts))
        sums[m] = sum(parts)


def surround(dims, buffer, m, near, far):
    members, levels, rows, halves, total_rows = dims
    tile = lax.axis_index("tile")
    odd = lax.rem(tile, 2) == 1
    first, last = tile == 0, tile == lax.axis_size("tile") - 1
    end = TILE + rows
    for f in range(4):
        for l in range(levels):
            for h in range(halves):
                index = (f, l, slice(None), half(h))
                a, b = near(index), far(index)
                buffer[m, f, l, h, TILE - WIDTH : TILE, :] = jnp.where(first, 0.0, jnp.where(odd, a, b))
                buffer[m, f, l, h, end : end + WIDTH, :] = jnp.where(last, 0.0, jnp.where(odd, b, a))


def outer_step(dims, source, target, m):
    members, levels, rows, halves, total_rows = dims
    tile = lax.axis_index("tile")
    row = lax.broadcasted_iota(jnp.int32, (TILE, LANES), 0)
    below = jnp.logical_and(tile == 0, row < REACH)
    above = jnp.logical_and(tile == lax.axis_size("tile") - 1, row >= TILE - REACH)
    for start, beyond in ((TILE - REACH, below), (rows + REACH, above)):
        sweep(dims, source, target, m, (start,), lambda f, l, h, start, value: jnp.where(beyond, 0.0, value))


def outer_early_kernel(dims, facing, halo, other_halo, mark, noise, zero_in, one_in, two_in, to_next, zero, one, two):
    members, levels, rows, halves, total_rows = dims
    tile = lax.axis_index("tile")
    low = lax.rem(tile, 2) == facing
    limit = jnp.where(low, 0, lax.axis_size("tile") - 1)
    row = lax.broadcasted_iota(jnp.int32, (TILE, LANES), 0)
    side = jnp.where(low, row, TILE - 1 - row)
    beyond = jnp.logical_and(tile == limit, side < REACH)

    def at(below, above):
        return jnp.where(low, below, above)

    for m in range(members):
        place = mark[m, :WIDTH, :]
        for f in range(4):
            for l in range(levels):
                for h in range(halves):
                    value = halo[0, f, l, :, half(h)]
                    for k in range(1, 2 * members):
                        array = halo if k < members else other_halo
                        value = jnp.where(place == k, array[k % members, f, l, :, half(h)], value)
                    value = jnp.where(tile == limit, 0.0, value)
                    zero[m, f, l, h, pl.ds(at(TILE - WIDTH, TILE + rows), WIDTH), :] = value
    for m in range(members):
        sweep(dims, zero, one, m, (at(TILE - REACH, rows + REACH),),
              lambda f, l, h, start, value: jnp.where(beyond, 0.0, value))
        sweep(dims, one, two, m, (at(TILE, rows),), perturbed(noise, m))
        for f in range(4):
            for l in range(levels):
                for h in range(halves):
                    to_next[m, f, l, :, half(h)] = two[m, f, l, h, pl.ds(at(TILE, TILE + rows - WIDTH), WIDTH), :]


def outer_late_kernel(dims, pair, cross, sums, two_in, three_in, zero_in, total, two, three, zero):
    members, levels, rows, halves, total_rows = dims
    sublane = lax.broadcasted_iota(jnp.int32, (TILE, LANES), 0)
    held = jnp.zeros((TILE, LANES), jnp.float32)
    for m in range(members):
        surround(dims, two, m, lambda index: pair[(m, *index)], lambda index: cross[(m, *index)])
    for m in range(members):
        outer_step(dims, two, three, m)
        parts = [sums[m]]
        sweep(dims, three, zero, m, (TILE, rows), weighed(dims, parts))
        column_sums = jnp.sum(sum(parts), axis=0, keepdims=True) * (1.0 / (levels * total_rows * halves * LANES))
        held = jnp.where(sublane == m, column_sums, held)
    total[...] = held


def place_kernel(dims, zero, fields, sems):
    members, levels, rows, halves, total_rows = dims
    started = []
    for m in range(members):
        started += result_copies(dims, zero, fields, sems, 0, m, TILE, rows)
    for copy in started:
        copy.start()
    for copy in started:
        copy.wait()


def tile_sum(value, count):
    if count & (count - 1):
        return lax.psum(value, "tile")
    reach = count // 2
    while reach:
        value = value + lax.ppermute(value, "tile", [(i, i ^ reach) for i in range(count)])
        reach //= 2
    return value


def body(state, perturbation, ancestors):
    members, _, levels, rows, columns = state.shape
    halves = columns // LANES
    count, groups = lax.axis_size("tile"), lax.axis_size("groups")
    dims = (members, levels, rows, halves, rows * count)
    f32 = jnp.float32

    def to_pair(array):
        return lax.ppermute(array, "tile", [(i, i ^ 1) for i in range(count)])

    def to_cross(array):
        def partner(group, i):
            if i in (0, count - 1):
                return (group ^ 1) * count + i if groups % 2 == 0 else group * count + count - 1 - i
            return group * count + (i + 1 if i % 2 else i - 1)

        pairs = [(group * count + i, partner(group, i)) for group in range(groups) for i in range(count)]
        return lax.ppermute(array, ("groups", "tile"), pairs)

    def to_member(array):
        return lax.ppermute(array, "member", [(0, 1), (1, 0)])

    def in_hbm(array):
        return pltpu.with_memory_space_constraint(array, pltpu.HBM)

    def spec(space):
        return pl.BlockSpec(memory_space=space)

    vmem, anywhere = spec(pltpu.VMEM), spec(pl.ANY)
    params = pltpu.CompilerParams(vmem_limit_bytes=VMEM_LIMIT)
    cells = state.size

    def cost(part):
        return pl.CostEstimate(flops=cells * part, bytes_accessed=cells * part, transcendentals=0)

    buffer = jax.ShapeDtypeStruct((members, 4, levels, halves, rows + 2 * TILE, LANES), f32)
    tile = jax.ShapeDtypeStruct((members, TILE, LANES), f32)
    strip = jax.ShapeDtypeStruct((members, 4, levels, WIDTH, columns), f32)

    other = to_member(state)
    edge_pair, edge_cross = pl.pallas_call(
        functools.partial(edge_kernel, dims),
        out_shape=(strip, strip),
        in_specs=[vmem, vmem],
        out_specs=(vmem, vmem),
        compiler_params=params,
        cost_estimate=cost(0),
        name="edge",
    )(state[:, :, :, :WIDTH], state[:, :, :, rows - WIDTH :])
    pair, cross = to_pair(edge_pair), to_cross(edge_cross)
    mark, zero, one, two, noise = pl.pallas_call(
        functools.partial(inner_early_kernel, dims),
        out_shape=(jax.ShapeDtypeStruct(tile.shape, jnp.int32),) + (buffer,) * 4,
        in_specs=[anywhere] * 4,
        out_specs=(vmem,) * 5,
        scratch_shapes=[
            pltpu.SMEM(ancestors.shape, jnp.int32),
            pltpu.SemaphoreType.DMA((2, members, halves)),
            pltpu.SemaphoreType.DMA,
        ],
        compiler_params=pltpu.CompilerParams(vmem_limit_bytes=WIDE_LIMIT),
        cost_estimate=cost(20),
        name="inner_early",
    )(in_hbm(ancestors), in_hbm(state), other, in_hbm(perturbation))
    pair, cross, mark = lax.optimization_barrier((pair, cross, mark))
    other_pair, other_cross = to_member(pair), to_member(cross)

    def outer_early(facing, halo, other_halo, zero, one, two):
        return pl.pallas_call(
            functools.partial(outer_early_kernel, dims, facing),
            out_shape=(strip,) + (buffer,) * 3,
            in_specs=[vmem] * 7,
            out_specs=(vmem,) * 4,
            input_output_aliases={4: 1, 5: 2, 6: 3},
            compiler_params=params,
            cost_estimate=cost(5),
            name="outer_early",
        )(halo, other_halo, mark, noise, zero, one, two)

    edge_pair, zero, one, two = outer_early(1, pair, other_pair, zero, one, two)
    pair = to_pair(edge_pair)
    edge_cross, zero, one, two = outer_early(0, cross, other_cross, zero, one, two)
    cross = to_cross(edge_cross)
    result = jax.ShapeDtypeStruct(state.shape, f32)
    sums, three, zero = pl.pallas_call(
        functools.partial(inner_late_kernel, dims),
        out_shape=(tile, buffer, buffer),
        in_specs=[vmem],
        out_specs=(vmem,) * 3,
        compiler_params=params,
        cost_estimate=cost(20),
        name="inner_late",
    )(two)
    pair, cross, sums = lax.optimization_barrier((pair, cross, sums))
    total, _, _, zero = pl.pallas_call(
        functools.partial(outer_late_kernel, dims),
        out_shape=(jax.ShapeDtypeStruct((TILE, LANES), f32),) + (buffer,) * 3,
        in_specs=[vmem] * 6,
        out_specs=(vmem,) * 4,
        input_output_aliases={3: 1, 4: 2, 5: 3},
        compiler_params=params,
        cost_estimate=cost(5),
        name="outer_late",
    )(pair, cross, sums, two, three, zero)
    evolved = pl.pallas_call(
        functools.partial(place_kernel, dims),
        out_shape=result,
        in_specs=[vmem],
        out_specs=anywhere,
        scratch_shapes=[pltpu.SemaphoreType.DMA((1, members, halves))],
        compiler_params=params,
        cost_estimate=cost(5),
        name="place",
    )(zero)
    observable = jnp.sum(tile_sum(total, count), axis=1)[:members]
    return evolved, observable


def solution(mesh):
    return jax.shard_map(
        body,
        mesh=mesh,
        in_specs=(
            P(("groups", "member"), None, None, "tile", None),
            P(("groups", "member"), None, None, "tile", None),
            P("groups"),
        ),
        out_specs=(P(("groups", "member"), None, None, "tile", None), P(("groups", "member"))),
        check_vma=False,
    )
```
